32 devices in a mesh: grp: 4 (over y, x), dev: 8 (over z, core).
Axes of the slice: x: 2, y: 2, z: 4, core: 2. Of those that a mesh axis runs over, the one named last changes fastest.
Arguments:
- queries: bfloat16 [8192, 4096], P(('grp', 'dev')), may hold values from -500 to 500
- new_kv: bfloat16 [8192, 2048], P(('grp', 'dev')), may hold values from -6 to 6
- kv_pool: bfloat16 [2048, 16, 2048], P(('grp', 'dev')), may hold values from -6 to 6
- hit_holder: int32 [32, 24], P(('grp', 'dev')), may hold values from 0 to 31, as said below
- hit_block: int32 [32, 24], P(('grp', 'dev')), may hold values from 0 to 63
- hit_count: int32 [32], P(('grp', 'dev')), may hold values from 12 to 24
- ssm_input: bfloat16 [8192, 8192], P(('grp', 'dev')), may hold values from -6 to 6
- step_size: float32 [8192, 128], P(('grp', 'dev')), may hold values from 0.04 to 0.16
- decay_rate: float32 [128], replicated, may hold values from 0.01 to 0.4
- state_in: float32 [8192, 16], P(('grp', 'dev')), may hold values from -6 to 6
- state_out: float32 [8192, 16], P(('grp', 'dev')), may hold values from -6 to 6
- skip_gain: float32 [128], replicated, may hold values from 0.1 to 1.9
- state_pool: float32 [64, 16, 8192], P(('grp', 'dev')), may hold values from -3 to 3
- state_group: int32 [32], P(('grp', 'dev')), may hold values from 0 to 3
- state_slot: int32 [32], P(('grp', 'dev')), may hold values from 0 to 1
Outputs:
- attended: bfloat16 [8192, 4096], P(('grp', 'dev'))
- mixed: bfloat16 [8192, 8192], P(('grp', 'dev'))
The draws below stay inside these ranges and needn't reach their ends.
Inputs may be any that keep to these rules, and one draw needn't show every extreme that they name: `hit_holder`: the first hit_count entries of a row name different holder devices.
All inputs are finite; a program needn't handle non-finite values.
Results may differ from the reference program's by a relative error of at most 0.0027.
Values may be sent and summed in bfloat16 or wider, within the bound.
No kernel may reach another device: no remote copies, remote signals or barrier semaphores. Data moves between devices by JAX's collectives and lax.ppermute only.
A program may use at most 256 MiB of HBM per device.

```python
import jax
import jax.numpy as jnp
from jax import lax

D = 4096
HEADS = 32
KV_HEADS = 8
HEAD_DIM = 128
DI = 8192
NS = 16
SSM_HEAD_DIM = 64
SSM_HEADS = 128
KVW = 2048
SUF = 256
BLK = 16
POOL = 64
SLOTS = 2
HIT_MAX = 24
TOKENS = 8192
N_GRP = 4
N_DEV = 8
DEVICES = 32


def draw_queries(key, part):
    base = jax.random.normal(key, (TOKENS, D), jnp.float32) * 3.0
    return jnp.clip(base, -500.0, 500.0).astype(jnp.bfloat16)


def draw_decay_rate(key, part):
    unit = jax.random.uniform(key, (SSM_HEADS,), jnp.float32)
    return jnp.exp(jnp.log(0.01) + unit * (jnp.log(0.4) - jnp.log(0.01)))


def draw_hit_holder(key, part):
    keys = jax.random.split(key, DEVICES)
    return jax.vmap(lambda k: jax.random.permutation(k, DEVICES)[:HIT_MAX])(keys).astype(jnp.int32)


def draw_hit_count(key, part):
    counts = jax.random.randint(key, (DEVICES,), HIT_MAX // 2, HIT_MAX + 1, jnp.int32)
    fullest = jax.random.randint(jax.random.fold_in(key, 1), (), 0, DEVICES, jnp.int32)
    return counts.at[fullest].set(HIT_MAX)


def set_ends(values, key, low, largest):
    longest = values.shape.index(max(values.shape))
    spots = []
    for shift in (0, 1):
        where = [jax.random.randint(jax.random.fold_in(key, axis), (), 0, length) for axis, length in enumerate(values.shape)]
        where[longest] = (where[longest] + shift) % values.shape[longest]
        spots.append(tuple(where))
    return values.at[spots[0]].set(low).at[spots[1]].set(largest)


def block_scale(own_key, extent, cuts, smallest, largest):
    def one(position, shards_of):
        heights = jax.random.uniform(jax.random.fold_in(jax.random.fold_in(own_key, 6), position), (shards_of,), jnp.float32, smallest / len(cuts), largest / len(cuts))
        return jnp.repeat(jnp.exp(heights), extent[position] // shards_of).reshape((-1,) + (1,) * (len(extent) - position - 1))

    factor_of = one(*cuts[0])
    for cut in cuts[1:]:
        factor_of = factor_of * one(*cut)
    return factor_of


def centred(stream_key, extent, deviation, limit, shards=(), kind=jnp.bfloat16):
    drawn = jax.random.normal(stream_key, extent, jnp.float32) * deviation
    if len(shards) > 0:
        drawn = block_scale(stream_key, extent, shards, -0.22, 0.18) * drawn
    return jnp.clip(drawn, min=-limit, max=limit).astype(kind)


def setup_inputs(seed: int = 0) -> dict:
    arg_keys = jax.random.split(jax.random.key(seed), 16)
    return {
        "queries": draw_queries(jax.random.fold_in(arg_keys[15], 71), 0),
        "new_kv": centred(arg_keys[1], (TOKENS, KVW), 1.0, 6.0, ((0, 32),)),
        "kv_pool": centred(arg_keys[2], (DEVICES * POOL, BLK, KVW), 1.0, 6.0, ((0, 32),)),
        "hit_holder": draw_hit_holder(jax.random.fold_in(arg_keys[15], 71), 0),
        "hit_block": set_ends(jax.random.randint(arg_keys[4], (DEVICES, HIT_MAX), 0, POOL), jax.random.fold_in(arg_keys[4], 1), 0, POOL - 1).astype(jnp.int32),
        "hit_count": draw_hit_count(jax.random.fold_in(arg_keys[15], 71), 0),
        "ssm_input": centred(arg_keys[6], (TOKENS, DI), 1.0, 6.0, ((0, 32),)),
        "step_size": jnp.clip(0.04 + 0.12 * jax.random.uniform(arg_keys[7], (TOKENS, SSM_HEADS), jnp.float32) ** block_scale(arg_keys[7], (TOKENS, SSM_HEADS), ((0, 32),), -0.2, 0.2), 0.04, 0.16),
        "decay_rate": draw_decay_rate(jax.random.fold_in(arg_keys[15], 71), 0),
        "state_in": centred(arg_keys[9], (TOKENS, NS), 1.0, 6.0, ((0, 32),), jnp.float32),
        "state_out": centred(arg_keys[10], (TOKENS, NS), 1.0, 6.0, ((0, 32),), jnp.float32),
        "skip_gain": jnp.clip(1.0 + 0.18 * jax.random.normal(arg_keys[11], (SSM_HEADS,), jnp.float32), 0.1, 1.9),
        "state_pool": centred(arg_keys[12], (DEVICES * SLOTS, NS, DI), 0.5, 3.0, ((0, 32),), jnp.float32),
        "state_group": set_ends(jax.random.randint(arg_keys[13], (DEVICES,), 0, N_GRP), jax.random.fold_in(arg_keys[13], 1), 0, N_GRP - 1).astype(jnp.int32),
        "state_slot": set_ends(jax.random.randint(arg_keys[14], (DEVICES,), 0, SLOTS), jax.random.fold_in(arg_keys[14], 1), 0, SLOTS - 1).astype(jnp.int32),
    }


def attend_one(qrows, keys_all, allowed):
    group = HEADS // KV_HEADS
    length = keys_all.shape[0]
    qh = qrows.reshape(SUF, KV_HEADS, group, HEAD_DIM).astype(jnp.float32)
    keys = keys_all[:, :KV_HEADS * HEAD_DIM].reshape(length, KV_HEADS, HEAD_DIM).astype(jnp.float32)
    values = keys_all[:, KV_HEADS * HEAD_DIM:].reshape(length, KV_HEADS, HEAD_DIM).astype(jnp.float32)
    scores = jnp.einsum("qhgd,khd->hgqk", qh, keys) * (HEAD_DIM ** -0.5)
    scores = jnp.where(allowed[None, None], scores, -1e30)
    top = jnp.max(scores, axis=-1, keepdims=True)
    weights = jnp.exp(scores - top)
    total = jnp.sum(weights, axis=-1)
    rounded = weights.astype(jnp.bfloat16).astype(jnp.float32)
    numer = jnp.einsum("hgqk,khd->qhgd", rounded, values)
    result = numer / jnp.transpose(total, (2, 0, 1))[:, :, :, None]
    return result.reshape(SUF, HEADS * HEAD_DIM).astype(jnp.bfloat16)


def reference(queries, new_kv, kv_pool, hit_holder, hit_block, hit_count, ssm_input, step_size, decay_rate, state_in, state_out, skip_gain, state_pool, state_group, state_slot):
    entries = jnp.arange(HIT_MAX, dtype=jnp.int32)
    positions = jnp.arange(SUF, dtype=jnp.int32)
    causal = positions[None, :] <= positions[:, None]

    def per_request(index):
        start = (index * SUF).astype(jnp.int32)
        qrows = lax.dynamic_slice_in_dim(queries, start, SUF, 0)
        own = lax.dynamic_slice_in_dim(new_kv, start, SUF, 0)
        rows = hit_holder[index] * POOL + hit_block[index]
        prefix = kv_pool[rows].reshape(HIT_MAX * BLK, KVW)
        live = jnp.repeat(entries < hit_count[index], BLK)
        keys_all = jnp.concatenate([prefix, own], axis=0)
        allowed = jnp.concatenate([jnp.broadcast_to(live[None, :], (SUF, HIT_MAX * BLK)), causal], axis=1)
        return attend_one(qrows, keys_all, allowed)

    attended = lax.map(per_request, jnp.arange(DEVICES, dtype=jnp.int32)).reshape(TOKENS, D)

    requester = jnp.arange(DEVICES, dtype=jnp.int32)
    where_state = (state_group * N_DEV + requester % N_DEV) * SLOTS + state_slot
    state = state_pool[where_state].reshape(DEVICES, NS, SSM_HEADS, SSM_HEAD_DIM)
    inputs = ssm_input.astype(jnp.float32).reshape(DEVICES, SUF, SSM_HEADS, SSM_HEAD_DIM)
    steps = step_size.reshape(DEVICES, SUF, SSM_HEADS)
    bmap = state_in.reshape(DEVICES, SUF, NS)
    cmap = state_out.reshape(DEVICES, SUF, NS)

    def advance(carry, slices):
        x_t, dt_t, b_t, c_t = slices
        factor = jnp.exp(-decay_rate[None, :] * dt_t)
        carry = factor[:, None, :, None] * carry + b_t[:, :, None, None] * (dt_t[:, :, None] * x_t)[:, None]
        y_t = jnp.einsum("rn,rnhp->rhp", c_t, carry, precision=lax.Precision.HIGHEST) + skip_gain[None, :, None] * x_t
        return carry, y_t

    slices = (jnp.swapaxes(inputs, 0, 1), jnp.swapaxes(steps, 0, 1), jnp.swapaxes(bmap, 0, 1), jnp.swapaxes(cmap, 0, 1))
    final, outputs = lax.scan(advance, state, slices)
    mixed = jnp.swapaxes(outputs, 0, 1).reshape(TOKENS, DI).astype(jnp.bfloat16)
    return attended, mixed
```

```python
import functools

import jax
import jax.numpy as jnp
from jax import lax
from jax.experimental import pallas as pl
from jax.experimental.pallas import tpu as pltpu
from jax.sharding import PartitionSpec as P

KV_HEADS = 8
HEAD_DIM = 128
SSM_HEAD_DIM = 64
LANES = 128
TILE = 1024
AXES = ("grp", "dev")
SCALE2 = HEAD_DIM ** (-0.5) * 1.4426950408889634
SMEM = pl.BlockSpec(memory_space=pltpu.SMEM)
ANY = pl.BlockSpec(memory_space=pl.ANY)
F32 = jnp.float32
BF16 = jnp.bfloat16


def params(megabytes=48):
    return pltpu.CompilerParams(vmem_limit_bytes=megabytes * 2**20)


def request_kernel(slots, holder, block, count, group, slot, out):
    rows = lax.broadcasted_iota(jnp.int32, out.shape, 0)
    lanes = lax.broadcasted_iota(jnp.int32, out.shape, 1)
    code = jnp.zeros(out.shape, jnp.int32)
    for j in range(holder.shape[1]):
        wanted = jnp.where(j < count[0], block[0, j], 0)
        code = jnp.where(rows == jnp.where(j < count[0], holder[0, j], -1), wanted, code)
    out[...] = jnp.where(lanes == 0, code, group[0] * slots + slot[0])


def make_requests(hit_holder, hit_block, hit_count, state_group, state_slot, n_all, slots):
    return pl.pallas_call(
        functools.partial(request_kernel, slots),
        out_shape=jax.ShapeDtypeStruct((n_all, LANES), jnp.int32),
        in_specs=[SMEM] * 5,
        out_specs=pl.BlockSpec(memory_space=pltpu.VMEM),
    )(hit_holder, hit_block, hit_count, state_group, state_slot)


def pick_kernel(asked, pool, out, held, in_sem, out_sem):
    n = out.shape[0]
    reads = [pltpu.make_async_copy(pool.at[asked[i, 0]], held.at[i], in_sem.at[i]) for i in range(n)]
    writes = [pltpu.make_async_copy(held.at[i], out.at[i], out_sem.at[i]) for i in range(n)]
    for copy in reads:
        copy.start()
    for read, write in zip(reads, writes):
        read.wait()
        write.start()
    for copy in writes:
        copy.wait()


def pick_blocks(asked, pool):
    n = asked.shape[0]
    shape = (n,) + pool.shape[1:]
    return pl.pallas_call(
        pick_kernel,
        out_shape=jax.ShapeDtypeStruct(shape, pool.dtype),
        in_specs=[SMEM, ANY],
        out_specs=ANY,
        scratch_shapes=[
            pltpu.VMEM(shape, pool.dtype),
            pltpu.SemaphoreType.DMA((n,)),
            pltpu.SemaphoreType.DMA((n,)),
        ],
        compiler_params=params(),
        cost_estimate=pl.CostEstimate(flops=0, bytes_accessed=4 * n * 65536, transcendentals=0),
    )(asked, pool)


def state_kernel(n_grp, n_dev, slots, place, asked, pool, *rest):
    outs, held, in_sem, out_sem = rest[:n_grp], rest[n_grp], rest[n_grp + 1], rest[n_grp + 2]
    reads = [pltpu.make_async_copy(pool.at[s], held.at[s], in_sem.at[s]) for s in range(slots)]
    for copy in reads:
        copy.start()
    for copy in reads:
        copy.wait()
    writes = []
    for shift in range(n_grp):
        row = lax.rem(place[0] + shift, n_grp) * n_dev + place[1]
        slot = lax.rem(asked[row, 1], slots)
        writes.append(pltpu.make_async_copy(held.at[slot], outs[shift], out_sem.at[shift]))
    for copy in writes:
        copy.start()
    for copy in writes:
        copy.wait()


def pick_states(asked, pool, place, n_grp, n_dev):
    slots = pool.shape[0]
    return pl.pallas_call(
        functools.partial(state_kernel, n_grp, n_dev, slots),
        out_shape=[jax.ShapeDtypeStruct(pool.shape[1:], pool.dtype)] * n_grp,
        in_specs=[SMEM, SMEM, ANY],
        out_specs=[ANY] * n_grp,
        scratch_shapes=[
            pltpu.VMEM(pool.shape, pool.dtype),
            pltpu.SemaphoreType.DMA((slots,)),
            pltpu.SemaphoreType.DMA((n_grp,)),
        ],
        compiler_params=params(),
        cost_estimate=pl.CostEstimate(flops=0, bytes_accessed=6 * 2**19, transcendentals=0),
    )(place, asked, pool)


def dot_nt(a, b):
    return lax.dot_general(a, b, (((1,), (1,)), ((), ())), preferred_element_type=F32)


def suffix_kernel(q, k, v, acc, stats):
    rows, group = q.shape[0], q.shape[1] // HEAD_DIM
    seen = lax.broadcasted_iota(jnp.int32, (rows, rows), 0) >= lax.broadcasted_iota(
        jnp.int32, (rows, rows), 1
    )
    lanes = lax.broadcasted_iota(jnp.int32, (rows, LANES), 1)
    packed = jnp.zeros((rows, LANES), F32)
    for g in range(group):
        cols = slice(g * HEAD_DIM, (g + 1) * HEAD_DIM)
        scores = jnp.where(seen, dot_nt(q[:, cols], k[...]), -1e30)
        top = jnp.max(scores, axis=1, keepdims=True)
        weights = jnp.exp2((scores - top) * SCALE2)
        total = jnp.sum(weights, axis=1, keepdims=True)
        acc[:, cols] = jnp.dot(weights.astype(BF16), v[...], preferred_element_type=F32)
        packed = jnp.where(lanes == g, top, packed)
        packed = jnp.where(lanes == group + g, total, packed)
    stats[0] = packed


def prefix_kernel(holder, count, q, k, v, acc, stats, out, keys, values):
    group, hits = q.shape[1] // HEAD_DIM, holder.shape[1]
    blk = k.shape[1]
    for j in range(hits):
        rows = slice(j * blk, (j + 1) * blk)
        keys[rows] = k[holder[0, j]]
        values[rows] = v[holder[0, j]]
    live = lax.broadcasted_iota(jnp.int32, (1, hits * blk), 1) < count[0] * blk
    packed = stats[0]
    for g in range(group):
        cols = slice(g * HEAD_DIM, (g + 1) * HEAD_DIM)
        scores = jnp.where(live, dot_nt(q[:, cols], keys[...]), -1e30)
        old_top = packed[:, g : g + 1]
        top = jnp.maximum(old_top, jnp.max(scores, axis=1, keepdims=True))
        weights = jnp.exp2((scores - top) * SCALE2)
        keep = jnp.exp2((old_top - top) * SCALE2)
        total = keep * packed[:, group + g : group + g + 1] + jnp.sum(weights, axis=1, keepdims=True)
        mixed = keep * acc[:, cols] + jnp.dot(
            weights.astype(BF16), values[...], preferred_element_type=F32
        )
        out[:, cols] = (mixed / total).astype(BF16)


def suffix_attention(queries, new_kv):
    rows, width = queries.shape
    span = width // KV_HEADS
    return pl.pallas_call(
        suffix_kernel,
        grid=(KV_HEADS,),
        out_shape=[
            jax.ShapeDtypeStruct((rows, width), F32),
            jax.ShapeDtypeStruct((KV_HEADS, rows, LANES), F32),
        ],
        in_specs=[
            pl.BlockSpec((rows, span), lambda i: (0, i)),
            pl.BlockSpec((rows, HEAD_DIM), lambda i: (0, i)),
            pl.BlockSpec((rows, HEAD_DIM), lambda i: (0, KV_HEADS + i)),
        ],
        out_specs=[
            pl.BlockSpec((rows, span), lambda i: (0, i)),
            pl.BlockSpec((1, rows, LANES), lambda i: (i, 0, 0)),
        ],
        compiler_params=params(),
        cost_estimate=pl.CostEstimate(
            flops=4 * rows * rows * width, bytes_accessed=8 * rows * width, transcendentals=rows * rows * 32
        ),
    )(queries, new_kv, new_kv)


def prefix_attention(queries, arrived, acc, stats, hit_holder, hit_count):
    rows, width = queries.shape
    n, blk, _ = arrived.shape
    span = width // KV_HEADS
    keys = hit_holder.shape[1] * blk
    return pl.pallas_call(
        prefix_kernel,
        grid=(KV_HEADS,),
        out_shape=jax.ShapeDtypeStruct((rows, width), BF16),
        in_specs=[
            SMEM,
            SMEM,
            pl.BlockSpec((rows, span), lambda i: (0, i)),
            pl.BlockSpec((n, blk, HEAD_DIM), lambda i: (0, 0, i)),
            pl.BlockSpec((n, blk, HEAD_DIM), lambda i: (0, 0, KV_HEADS + i)),
            pl.BlockSpec((rows, span), lambda i: (0, i)),
            pl.BlockSpec((1, rows, LANES), lambda i: (i, 0, 0)),
        ],
        out_specs=pl.BlockSpec((rows, span), lambda i: (0, i)),
        scratch_shapes=[pltpu.VMEM((keys, HEAD_DIM), BF16), pltpu.VMEM((keys, HEAD_DIM), BF16)],
        compiler_params=params(),
        cost_estimate=pl.CostEstimate(
            flops=4 * rows * keys * width, bytes_accessed=8 * rows * width, transcendentals=rows * keys * 32
        ),
    )(hit_holder, hit_count, queries, arrived, arrived, acc, stats)


def two_parts(value):
    high = value.astype(BF16)
    return high, (value - high.astype(F32)).astype(BF16)


def mixer_kernel(n_grp, choice, x, step, rate, into, outof, gain, *rest):
    states, y = rest[:n_grp], rest[n_grp]
    wide, inner, carried, start, sem = rest[n_grp + 1 :]
    rows, heads = step.shape
    index = pl.program_id(0)

    @pl.when(index == 0)
    def prepare():
        for shift in range(n_grp):

            @pl.when(choice[0] == shift)
            def fetch(shift=shift):
                pltpu.make_async_copy(states[shift], start, sem).start()

        lower = lax.broadcasted_iota(jnp.int32, (rows, rows), 0) >= lax.broadcasted_iota(
            jnp.int32, (rows, rows), 1
        )
        decay = jnp.dot(
            lower.astype(F32), -rate[...] * step[...], precision=lax.Precision.HIGHEST,
            preferred_element_type=F32,
        )
        rise = jnp.exp(decay)
        fall = jnp.exp(-decay) * step[...]
        wide[:rows, :heads], wide[:rows, heads:] = two_parts(rise)
        wide[rows : 2 * rows, :heads], wide[rows : 2 * rows, heads:] = two_parts(fall)
        gains = jnp.broadcast_to(gain[...], (16, heads))
        wide[2 * rows :, :heads], wide[2 * rows :, heads:] = two_parts(gains)
        cross = lax.dot_general(
            outof[...], into[...], (((1,), (1,)), ((), ())),
            precision=lax.Precision.HIGHEST, preferred_element_type=F32,
        )
        high, low = two_parts(jnp.where(lower, cross, 0.0))
        inner[:, :rows] = high
        inner[:, rows : 2 * rows] = high
        inner[:, 2 * rows :] = low
        high, low = two_parts(outof[...])
        carried[...] = jnp.concatenate([high, high, low], axis=1)
        pltpu.make_async_copy(states[0], start, sem).wait()

    tile = x.shape[1]
    per_tile = tile // SSM_HEAD_DIM
    head_of = lax.broadcasted_iota(jnp.int32, (heads, tile), 1) // SSM_HEAD_DIM + index * per_tile
    spread = (lax.broadcasted_iota(jnp.int32, (heads, tile), 0) == head_of).astype(F32).astype(BF16)
    spread = jnp.concatenate([spread, spread], axis=0)
    expanded = jnp.dot(wide[...], spread, preferred_element_type=F32)
    values = x[...].astype(F32)
    high, low = two_parts(expanded[rows : 2 * rows] * values)
    total = jnp.dot(
        inner[...], jnp.concatenate([high, low, high], axis=0), preferred_element_type=F32
    )
    first = start[:, pl.ds(pl.multiple_of(index * tile, tile), tile)]
    high, low = two_parts(first)
    total = total + jnp.dot(
        carried[...], jnp.concatenate([high, low, high], axis=0), preferred_element_type=F32
    )
    y[...] = (expanded[:rows] * total + expanded[2 * rows : 2 * rows + 1] * values).astype(BF16)


def mixer(choice, ssm_input, step_size, decay_rate, state_in, state_out, skip_gain, states):
    rows, channels = ssm_input.shape
    heads, ns = decay_rate.shape[0], state_in.shape[1]
    n_grp = len(states)
    whole = lambda shape: pl.BlockSpec(shape, lambda i: (0,) * len(shape))
    return pl.pallas_call(
        functools.partial(mixer_kernel, n_grp),
        grid=(channels // TILE,),
        out_shape=jax.ShapeDtypeStruct((rows, channels), BF16),
        in_specs=[
            SMEM,
            pl.BlockSpec((rows, TILE), lambda i: (0, i)),
            whole((rows, heads)),
            whole((1, heads)),
            whole((rows, ns)),
            whole((rows, ns)),
            whole((1, heads)),
        ]
        + [ANY] * n_grp,
        out_specs=pl.BlockSpec((rows, TILE), lambda i: (0, i)),
        scratch_shapes=[
            pltpu.VMEM((2 * rows + 16, 2 * heads), BF16),
            pltpu.VMEM((rows, 3 * rows), BF16),
            pltpu.VMEM((rows, 3 * ns), BF16),
            pltpu.VMEM((ns, channels), F32),
            pltpu.SemaphoreType.DMA,
        ],
        compiler_params=params(),
        cost_estimate=pl.CostEstimate(
            flops=12 * rows * rows * channels, bytes_accessed=4 * rows * channels, transcendentals=0
        ),
    )(
        choice, ssm_input, step_size, decay_rate[None, :], state_in, state_out, skip_gain[None, :], *states
    )


def body(
    queries,
    new_kv,
    kv_pool,
    hit_holder,
    hit_block,
    hit_count,
    ssm_input,
    step_size,
    decay_rate,
    state_in,
    state_out,
    skip_gain,
    state_pool,
    state_group,
    state_slot,
):
    n_grp, n_dev = lax.axis_size("grp"), lax.axis_size("dev")
    n_all = n_grp * n_dev
    slots = state_pool.shape[0]
    own_group = lax.axis_index("grp").astype(jnp.int32)
    place = jnp.stack([own_group, lax.axis_index("dev").astype(jnp.int32)])
    requests = make_requests(
        hit_holder, hit_block, hit_count, state_group, state_slot, n_all, slots
    )
    asked = lax.all_to_all(requests, AXES, split_axis=0, concat_axis=0, tiled=True)
    acc, stats = suffix_attention(queries, new_kv)
    arrived = lax.all_to_all(
        pick_blocks(asked, kv_pool), AXES, split_axis=0, concat_axis=0, tiled=True
    )
    states = pick_states(asked, state_pool, place, n_grp, n_dev)
    states = [states[0]] + [
        lax.ppermute(states[s], "grp", [(i, (i + s) % n_grp) for i in range(n_grp)])
        for s in range(1, n_grp)
    ]
    choice = lax.rem(own_group - state_group + n_grp, n_grp)
    mixed = mixer(
        choice, ssm_input, step_size, decay_rate, state_in, state_out, skip_gain, states
    )
    attended = prefix_attention(queries, arrived, acc, stats, hit_holder, hit_count)
    return (attended, mixed)


def solution(mesh):
    spread = P(AXES, None)
    spread3 = P(AXES, None, None)
    line = P(AXES)
    return jax.shard_map(
        body,
        mesh=mesh,
        in_specs=(
            spread,
            spread,
            spread3,
            spread,
            spread,
            line,
            spread,
            spread,
            P(),
            spread,
            spread,
            P(),
            spread3,
            line,
            line,
        ),
        out_specs=(spread, spread),
        check_vma=False,
    )
```

```python
import functools

import jax
import jax.numpy as jnp
from jax import lax
from jax.experimental import pallas as pl
from jax.experimental.pallas import tpu as pltpu
from jax.sharding import PartitionSpec as P

KV_HEADS = 8
HEAD_DIM = 128
SSM_HEAD_DIM = 64
LANES = 128
TILE = 1024
AXES = ("grp", "dev")
SCALE2 = HEAD_DIM ** (-0.5) * 1.4426950408889634
SMEM = pl.BlockSpec(memory_space=pltpu.SMEM)
VMEM = pl.BlockSpec(memory_space=pltpu.VMEM)
HBM = pl.BlockSpec(memory_space=pltpu.HBM)
MIB = 2**20
WHOLE = 56 * MIB
F32 = jnp.float32
BF16 = jnp.bfloat16


def params(limit):
    return pltpu.CompilerParams(vmem_limit_bytes=limit)


def request_kernel(slots, holder, block, count, group, slot, out):
    rows = lax.broadcasted_iota(jnp.int32, out.shape, 0)
    lanes = lax.broadcasted_iota(jnp.int32, out.shape, 1)
    code = jnp.zeros(out.shape, jnp.int32)
    for j in range(holder.shape[1]):
        wanted = jnp.where(j < count[0, 0], holder[0, j], -1)
        code = jnp.where(rows == wanted, block[0, j] + 1, code)
    out[...] = jnp.where(lanes == 0, code, group[0, 0] * slots + slot[0, 0])


def make_requests(hit_holder, hit_block, hit_count, state_group, state_slot, n_all, slots):
    one = lambda value: value.reshape(1, 1)
    return pl.pallas_call(
        functools.partial(request_kernel, slots),
        out_shape=jax.ShapeDtypeStruct((n_all, LANES), jnp.int32),
        in_specs=[SMEM] * 5,
        out_specs=VMEM,
    )(hit_holder, hit_block, one(hit_count), one(state_group), one(state_slot))


def pick_kernel(asked, pool, out, held, in_sem, out_sem):
    n = out.shape[0]

    def read(i):
        return pltpu.make_async_copy(pool.at[jnp.maximum(asked[i, 0] - 1, 0)], held.at[i], in_sem.at[i])

    def write(i):
        return pltpu.make_async_copy(held.at[i], out.at[i], out_sem.at[i])

    for i in range(n):
        pl.when(asked[i, 0] > 0)(lambda i=i: read(i).start())
    for i in range(n):

        @pl.when(asked[i, 0] > 0)
        def forward(i=i):
            read(i).wait()
            write(i).start()

    for i in range(n):
        pl.when(asked[i, 0] > 0)(lambda i=i: write(i).wait())


def pick_blocks(asked, pool):
    n = asked.shape[0]
    shape = (n,) + pool.shape[1:]
    return pl.pallas_call(
        pick_kernel,
        out_shape=jax.ShapeDtypeStruct(shape, pool.dtype),
        in_specs=[SMEM, HBM],
        out_specs=HBM,
        scratch_shapes=[
            pltpu.VMEM(shape, pool.dtype),
            pltpu.SemaphoreType.DMA((n,)),
            pltpu.SemaphoreType.DMA((n,)),
        ],
        compiler_params=params(WHOLE),
        cost_estimate=pl.CostEstimate(flops=0, bytes_accessed=4 * n * 65536, transcendentals=0),
    )(asked, pool)


def state_kernel(place, asked, pool, from_x, from_y, out_x, out_y, held, in_sem, out_sem):
    slots, early, own = pool.shape[0], from_x.shape[0], place[0]
    routes = []
    for number, (by, out) in enumerate(((1, out_x), (2, out_y))):
        code = asked[lax.bitwise_xor(own, by) * place[2] + place[1], 1]
        group, slot = lax.div(code, slots), lax.rem(code, slots)
        over_x = by == 1
        fits = slot >= early if over_x else slot < early
        here = fits & (group == own)
        beyond = fits & (group == lax.bitwise_xor(own, 3 - by))
        there, at = (from_y, slot - early) if over_x else (from_x, slot)
        routes.append((number, out, here, beyond, slot, there, at))

    def read(number, source):
        return pltpu.make_async_copy(source, held.at[number], in_sem.at[number])

    def write(number, out):
        return pltpu.make_async_copy(held.at[number], out, out_sem.at[number])

    for number, out, here, beyond, slot, there, at in routes:
        pl.when(here)(lambda n=number, slot=slot: read(n, pool.at[slot]).start())
        pl.when(beyond)(lambda n=number, there=there, at=at: read(n, there.at[at]).start())
    for number, out, here, beyond, *_ in routes:

        @pl.when(here | beyond)
        def forward(number=number, out=out):
            read(number, pool.at[0]).wait()
            write(number, out).start()

    for number, out, here, beyond, *_ in routes:
        pl.when(here | beyond)(lambda n=number, out=out: write(n, out).wait())


def neighbour_states(asked, pool, from_x, from_y, place):
    return pl.pallas_call(
        state_kernel,
        out_shape=[jax.ShapeDtypeStruct(pool.shape[1:], pool.dtype)] * 2,
        in_specs=[SMEM, SMEM, HBM, HBM, HBM],
        out_specs=[HBM, HBM],
        scratch_shapes=[
            pltpu.VMEM((2,) + pool.shape[1:], pool.dtype),
            pltpu.SemaphoreType.DMA((2,)),
            pltpu.SemaphoreType.DMA((2,)),
        ],
        compiler_params=params(WHOLE),
        cost_estimate=pl.CostEstimate(flops=0, bytes_accessed=2**20, transcendentals=0),
    )(place, asked, pool, from_x, from_y)


def dot_nt(a, b):
    return lax.dot_general(a, b, (((1,), (1,)), ((), ())), preferred_element_type=F32)


def suffix_kernel(q, k, v, acc, stats):
    rows, group = q.shape[0], q.shape[1] // HEAD_DIM
    stacked = jnp.concatenate([q[:, g * HEAD_DIM : (g + 1) * HEAD_DIM] for g in range(group)], axis=0)
    shape = (rows, group * rows)
    query = lax.rem(lax.broadcasted_iota(jnp.int32, shape, 1), rows)
    seen = lax.broadcasted_iota(jnp.int32, shape, 0) <= query
    scores = jnp.where(seen, dot_nt(k[...], stacked), -1e30)
    top = jnp.max(scores, axis=0, keepdims=True)
    weights = jnp.exp2((scores - top) * SCALE2)
    total = jnp.sum(weights, axis=0, keepdims=True)
    mixed = jnp.dot(v[...].T, weights.astype(BF16), preferred_element_type=F32)
    for g in range(group):
        cols = slice(g * rows, (g + 1) * rows)
        acc[g * HEAD_DIM : (g + 1) * HEAD_DIM] = mixed[:, cols]
        stats[0, g : g + 1] = top[:, cols]
        stats[0, group + g : group + g + 1] = total[:, cols]


def suffix_attention(queries, new_kv):
    rows, width = queries.shape
    span = width // KV_HEADS
    lines = 2 * span // HEAD_DIM
    return pl.pallas_call(
        suffix_kernel,
        grid=(KV_HEADS,),
        out_shape=[
            jax.ShapeDtypeStruct((width, rows), F32),
            jax.ShapeDtypeStruct((KV_HEADS, lines, rows), F32),
        ],
        in_specs=[
            pl.BlockSpec((rows, span), lambda i: (0, i)),
            pl.BlockSpec((rows, HEAD_DIM), lambda i: (0, i)),
            pl.BlockSpec((rows, HEAD_DIM), lambda i: (0, KV_HEADS + i)),
        ],
        out_specs=[
            pl.BlockSpec((span, rows), lambda i: (i, 0)),
            pl.BlockSpec((1, lines, rows), lambda i: (i, 0, 0)),
        ],
        compiler_params=params(WHOLE),
        cost_estimate=pl.CostEstimate(
            flops=4 * rows * rows * width, bytes_accessed=8 * rows * width, transcendentals=rows * rows * 32
        ),
    )(queries, new_kv, new_kv)


def prefix_kernel(
    holder, count, q_hbm, acc_hbm, stats_hbm, arrived, out,
    kv, q, acc, stats, res, k_sem, v_sem, q_sem, acc_sem, stats_sem, out_sem,
):
    hits, blk = holder.shape[0], arrived.shape[1]
    rows, width = q.shape
    span, keys, half = width // KV_HEADS, hits * blk, KV_HEADS * HEAD_DIM
    group = span // HEAD_DIM

    def from_holder(j, side, sem):
        source = jnp.where(j < count[0, 0], holder[j], holder[0])
        cols = pl.ds(side * half, half)
        return pltpu.make_async_copy(arrived.at[source, :, cols], kv.at[pl.ds(j * blk, blk), cols], sem.at[j])

    def queries_of(k):
        cols = pl.ds(k * span, span)
        return pltpu.make_async_copy(q_hbm.at[:, cols], q.at[:, cols], q_sem.at[k])

    def suffix_of(k):
        lines = pl.ds(k * span, span)
        return pltpu.make_async_copy(acc_hbm.at[lines], acc.at[lines], acc_sem.at[k])

    queries_of(0).start()
    for j in range(hits):
        from_holder(j, 0, k_sem).start()
    stats_copy = pltpu.make_async_copy(stats_hbm, stats, stats_sem)
    stats_copy.start()
    for j in range(hits):
        from_holder(j, 1, v_sem).start()
    suffix_of(0).start()
    queries_of(1).start()
    live = lax.broadcasted_iota(jnp.int32, (keys, 1), 0) < count[0, 0] * blk
    for j in range(hits):
        from_holder(j, 0, k_sem).wait()

    def scores_of(k):
        queries_of(k).wait()
        if k + 2 < KV_HEADS:
            queries_of(k + 2).start()
        if k + 1 < KV_HEADS:
            suffix_of(k + 1).start()
        stacked = [q[:, k * span + g * HEAD_DIM : k * span + (g + 1) * HEAD_DIM] for g in range(group)]
        return dot_nt(kv[:, k * HEAD_DIM : (k + 1) * HEAD_DIM], jnp.concatenate(stacked, axis=0))

    later = scores_of(0)
    stats_copy.wait()
    sends = []
    for k in range(KV_HEADS):
        scores = jnp.where(live, later, -1e30)
        if k + 1 < KV_HEADS:
            later = scores_of(k + 1)
        old = jnp.concatenate([stats[k, g : g + 1] for g in range(group)], axis=1)
        before = jnp.concatenate([stats[k, group + g : group + g + 1] for g in range(group)], axis=1)
        top = jnp.maximum(old, jnp.max(scores, axis=0, keepdims=True))
        weights = jnp.exp2((scores - top) * SCALE2)
        keep = jnp.exp2((old - top) * SCALE2)
        total = keep * before + jnp.sum(weights, axis=0, keepdims=True)
        if k == 0:
            for j in range(hits):
                from_holder(j, 1, v_sem).wait()
        head_values = kv[:, half + k * HEAD_DIM : half + (k + 1) * HEAD_DIM]
        mixed = jnp.dot(head_values.T, weights.astype(BF16), preferred_element_type=F32)
        inverse = 1.0 / total
        kept = keep * inverse
        suffix_of(k).wait()
        for g in range(group):
            lines = slice(k * span + g * HEAD_DIM, k * span + (g + 1) * HEAD_DIM)
            cols = slice(g * rows, (g + 1) * rows)
            both = kept[:, cols] * acc[lines] + inverse[:, cols] * mixed[:, cols]
            res[:, lines] = both.T.astype(BF16)
        cols = pl.ds(k * span, span)
        sends.append(pltpu.make_async_copy(res.at[:, cols], out.at[:, cols], out_sem.at[k]))
        sends[-1].start()
    for copy in sends:
        copy.wait()


def prefix_attention(queries, acc, stats, arrived, hit_holder, hit_count):
    rows, width = queries.shape
    blk, kv_width = arrived.shape[1:]
    hits = hit_holder.shape[0]
    keys = hits * blk
    dma = pltpu.SemaphoreType.DMA
    return pl.pallas_call(
        prefix_kernel,
        out_shape=jax.ShapeDtypeStruct((rows, width), BF16),
        in_specs=[SMEM, SMEM, HBM, HBM, HBM, HBM],
        out_specs=HBM,
        scratch_shapes=[
            pltpu.VMEM((keys, kv_width), BF16),
            pltpu.VMEM((rows, width), BF16),
            pltpu.VMEM((width, rows), F32),
            pltpu.VMEM(stats.shape, F32),
            pltpu.VMEM((rows, width), BF16),
            dma((hits,)),
            dma((hits,)),
            dma((KV_HEADS,)),
            dma((KV_HEADS,)),
            dma,
            dma((KV_HEADS,)),
        ],
        compiler_params=params(58 * MIB),
        cost_estimate=pl.CostEstimate(
            flops=4 * rows * keys * width, bytes_accessed=8 * rows * width, transcendentals=rows * keys * 32
        ),
    )(hit_holder, hit_count.reshape(1, 1), queries, acc, stats, arrived)


def two_parts(value):
    high = value.astype(BF16)
    return high, (value - high.astype(F32)).astype(BF16)


def spread_of(heads, tile):
    first = pl.program_id(0) * (tile // SSM_HEAD_DIM)
    head_of = lax.broadcasted_iota(jnp.int32, (heads, tile), 1) // SSM_HEAD_DIM + first
    same = lax.broadcasted_iota(jnp.int32, (heads, tile), 0) == head_of
    spread = same.astype(F32).astype(BF16)
    return jnp.concatenate([spread, spread], axis=0)


def mixer_kernel(choice, slot, x, step, rate, into, outof, gain, *rest):
    pools, states = rest[:3], rest[3:-6]
    y, wide, inner, carried, start, sem = rest[-6:]
    rows, heads = step.shape
    index = pl.program_id(0)

    @pl.when(index == 0)
    def prepare():
        sources = [pool.at[slot[0]] for pool in pools] + list(states)
        for shift, source in enumerate(sources):

            @pl.when(choice[0] == shift)
            def fetch(source=source):
                pltpu.make_async_copy(source, start, sem).start()

        lower = lax.broadcasted_iota(jnp.int32, (rows, rows), 0) >= lax.broadcasted_iota(
            jnp.int32, (rows, rows), 1
        )
        decay = jnp.dot(
            lower.astype(F32), -rate[...] * step[...], precision=lax.Precision.HIGHEST,
            preferred_element_type=F32,
        )
        rise = jnp.exp(decay)
        fall = jnp.exp(-decay) * step[...]
        wide[:rows, :heads], wide[:rows, heads:] = two_parts(rise)
        wide[rows : 2 * rows, :heads], wide[rows : 2 * rows, heads:] = two_parts(fall)
        gains = jnp.broadcast_to(gain[...], (16, heads))
        wide[2 * rows :, :heads], wide[2 * rows :, heads:] = two_parts(gains)
        cross = lax.dot_general(
            outof[...], into[...], (((1,), (1,)), ((), ())),
            precision=lax.Precision.HIGHEST, preferred_element_type=F32,
        )
        high, low = two_parts(jnp.where(lower, cross, 0.0))
        inner[:, :rows] = high
        inner[:, rows : 2 * rows] = high
        inner[:, 2 * rows :] = low
        high, low = two_parts(outof[...])
        carried[...] = jnp.concatenate([high, high, low], axis=1)
        pltpu.make_async_copy(pools[0].at[0], start, sem).wait()

    tile = x.shape[1]
    spread = spread_of(heads, tile)
    expanded = jnp.dot(wide[...], spread, preferred_element_type=F32)
    values = x[...].astype(F32)
    high, low = two_parts(expanded[rows : 2 * rows] * values)
    total = jnp.dot(
        inner[...], jnp.concatenate([high, low, high], axis=0), preferred_element_type=F32
    )
    first = start[:, pl.ds(pl.multiple_of(index * tile, tile), tile)]
    high, low = two_parts(first)
    total = total + jnp.dot(
        carried[...], jnp.concatenate([high, low, high], axis=0), preferred_element_type=F32
    )
    y[...] = (expanded[:rows] * total + expanded[2 * rows : 2 * rows + 1] * values).astype(BF16)


def mixer(choice, slot, ssm_input, step_size, decay_rate, state_in, state_out, skip_gain, pools, states):
    rows, channels = ssm_input.shape
    heads, ns = decay_rate.shape[0], state_in.shape[1]
    whole = lambda shape: pl.BlockSpec(shape, lambda i: (0,) * len(shape))
    return pl.pallas_call(
        mixer_kernel,
        grid=(channels // TILE,),
        out_shape=jax.ShapeDtypeStruct((rows, channels), BF16),
        in_specs=[
            SMEM,
            SMEM,
            pl.BlockSpec((rows, TILE), lambda i: (0, i)),
            whole((rows, heads)),
            whole((1, heads)),
            whole((rows, ns)),
            whole((rows, ns)),
            whole((1, heads)),
        ]
        + [HBM] * (len(pools) + len(states)),
        out_specs=pl.BlockSpec((rows, TILE), lambda i: (0, i)),
        scratch_shapes=[
            pltpu.VMEM((2 * rows + 16, 2 * heads), BF16),
            pltpu.VMEM((rows, 3 * rows), BF16),
            pltpu.VMEM((rows, 3 * ns), BF16),
            pltpu.VMEM((ns, channels), F32),
            pltpu.SemaphoreType.DMA,
        ],
        compiler_params=params(WHOLE),
        cost_estimate=pl.CostEstimate(
            flops=12 * rows * rows * channels, bytes_accessed=4 * rows * channels, transcendentals=0
        ),
    )(
        choice, slot, ssm_input, step_size, decay_rate[None, :], state_in, state_out, skip_gain[None, :], *pools, *states
    )


def body(
    queries,
    new_kv,
    kv_pool,
    hit_holder,
    hit_block,
    hit_count,
    ssm_input,
    step_size,
    decay_rate,
    state_in,
    state_out,
    skip_gain,
    state_pool,
    state_group,
    state_slot,
):
    n_grp, n_dev = lax.axis_size("grp"), lax.axis_size("dev")
    own_group = lax.axis_index("grp").astype(jnp.int32)
    own_dev = lax.axis_index("dev").astype(jnp.int32)
    place = jnp.stack([own_group, own_dev, jnp.int32(n_dev)])
    slots = state_pool.shape[0]
    early = slots - slots // 2

    def swap(value, by):
        return lax.ppermute(value, "grp", [(i, i ^ by) for i in range(n_grp)])

    near = n_grp == 4 and slots > 1
    requests = make_requests(hit_holder, hit_block, hit_count, state_group, state_slot, n_grp * n_dev, slots)
    asked = lax.all_to_all(requests, AXES, split_axis=0, concat_axis=0, tiled=True)
    if near:
        from_x, from_y = swap(state_pool[:early], 1), swap(state_pool[early:], 2)
        asked, from_x, from_y = lax.optimization_barrier((asked, from_x, from_y))
    picked = pick_blocks(asked, kv_pool)
    arrived = lax.all_to_all(picked, AXES, split_axis=0, concat_axis=0, tiled=True)
    if near:
        out_x, out_y = neighbour_states(asked, state_pool, from_x, from_y, place)
        pools, states = (state_pool, from_x, from_y), (swap(out_x, 1), swap(out_y, 2))
        first = state_slot < early
        step = lax.bitwise_xor(own_group, state_group)
        far = jnp.where(first, jnp.where(step == 1, 1, 4), jnp.where(step == 2, 2, 3))
        choice = jnp.where(step == 0, 0, far)
        slot = jnp.where(choice == 2, state_slot - early, state_slot)
    else:
        everyone = lax.all_gather(state_pool, "grp", axis=0, tiled=True)
        pools, states = (everyone,) * 3, ()
        choice, slot = jnp.zeros_like(state_slot), state_group * slots + state_slot
    acc, stats = suffix_attention(queries, new_kv)
    mixed = mixer(
        choice, slot, ssm_input, step_size, decay_rate, state_in, state_out, skip_gain, pools, states
    )
    attended = prefix_attention(queries, acc, stats, arrived, hit_holder[0], hit_count)
    return (attended, mixed)


def solution(mesh):
    spread = P(AXES, None)
    spread3 = P(AXES, None, None)
    line = P(AXES)
    return jax.shard_map(
        body,
        mesh=mesh,
        in_specs=(
            spread,
            spread,
            spread3,
            spread,
            spread,
            line,
            spread,
            spread,
            P(),
            spread,
            spread,
            P(),
            spread3,
            line,
            line,
        ),
        out_specs=(spread, spread),
        check_vma=False,
    )
```

```python
import functools

import jax
import jax.numpy as jnp
from jax import lax
from jax.experimental import pallas as pl
from jax.experimental.pallas import tpu as pltpu
from jax.sharding import PartitionSpec as P

KV_HEADS = 8
HEAD_DIM = 128
SSM_HEAD_DIM = 64
LANES = 128
TILE = 1024
AXES = ("grp", "dev")
SCALE2 = HEAD_DIM ** (-0.5) * 1.4426950408889634
SMEM = pl.BlockSpec(memory_space=pltpu.SMEM)
VMEM = pl.BlockSpec(memory_space=pltpu.VMEM)
HBM = pl.BlockSpec(memory_space=pltpu.HBM)
MIB = 2**20
ROOM = 8
WHOLE = 56 * MIB
F32 = jnp.float32
BF16 = jnp.bfloat16


def params(limit):
    return pltpu.CompilerParams(vmem_limit_bytes=limit)


def request_kernel(slots, holder, block, count, group, slot, out):
    shape = (out.shape[0], holder.shape[1])
    rows = lax.broadcasted_iota(jnp.int32, shape, 0)
    entries = lax.broadcasted_iota(jnp.int32, shape, 1)
    chosen = (rows == holder[...]) & (entries < count[...])
    code = jnp.sum(jnp.where(chosen, block[...] + 1, 0), axis=1, keepdims=True)
    lanes = lax.broadcasted_iota(jnp.int32, out.shape, 1)
    out[...] = jnp.where(lanes == 0, code, group[...] * slots + slot[...])


def make_requests(hit_holder, hit_block, hit_count, state_group, state_slot, n_all, slots):
    one = lambda value: value.reshape(1, 1)
    return pl.pallas_call(
        functools.partial(request_kernel, slots),
        out_shape=jax.ShapeDtypeStruct((n_all, LANES), jnp.int32),
        in_specs=[VMEM] * 5,
        out_specs=VMEM,
    )(hit_holder, hit_block, one(hit_count), one(state_group), one(state_slot))


def pick_kernel(asked, pool, out, held, in_sem, out_sem):
    n = out.shape[0]

    def read(i):
        return pltpu.make_async_copy(pool.at[jnp.maximum(asked[i, 0] - 1, 0)], held.at[i], in_sem.at[i])

    def write(i):
        return pltpu.make_async_copy(held.at[i], out.at[i], out_sem.at[i])

    for i in range(n):
        pl.when(asked[i, 0] > 0)(lambda i=i: read(i).start())
    for i in range(n):

        @pl.when(asked[i, 0] > 0)
        def forward(i=i):
            read(i).wait()
            write(i).start()

    for i in range(n):
        pl.when(asked[i, 0] > 0)(lambda i=i: write(i).wait())


def pick_blocks(asked, pool):
    n = asked.shape[0]
    shape = (n,) + pool.shape[1:]
    return pl.pallas_call(
        pick_kernel,
        out_shape=jax.ShapeDtypeStruct(shape, pool.dtype),
        in_specs=[SMEM, HBM],
        out_specs=HBM,
        scratch_shapes=[
            pltpu.VMEM(shape, pool.dtype),
            pltpu.SemaphoreType.DMA((n,)),
            pltpu.SemaphoreType.DMA((n,)),
        ],
        compiler_params=params(WHOLE),
        cost_estimate=pl.CostEstimate(flops=0, bytes_accessed=4 * n * 65536, transcendentals=0),
    )(asked, pool)


def state_kernel(place, asked, pool, from_x, from_y, out_x, out_y, held, in_sem, out_sem):
    slots, early, own = pool.shape[0], from_x.shape[0], place[0]
    routes = []
    for number, (by, out) in enumerate(((1, out_x), (2, out_y))):
        code = asked[lax.bitwise_xor(own, by) * place[2] + place[1], 1]
        group, slot = lax.div(code, slots), lax.rem(code, slots)
        over_x = by == 1
        fits = slot >= early if over_x else slot < early
        here = fits & (group == own)
        beyond = fits & (group == lax.bitwise_xor(own, 3 - by))
        there, at = (from_y, slot - early) if over_x else (from_x, slot)
        routes.append((number, out, here, beyond, slot, there, at))

    def read(number, source):
        return pltpu.make_async_copy(source, held.at[number], in_sem.at[number])

    def write(number, out):
        return pltpu.make_async_copy(held.at[number], out, out_sem.at[number])

    for number, out, here, beyond, slot, there, at in routes:
        pl.when(here)(lambda n=number, slot=slot: read(n, pool.at[slot]).start())
        pl.when(beyond)(lambda n=number, there=there, at=at: read(n, there.at[at]).start())
    for number, out, here, beyond, *_ in routes:

        @pl.when(here | beyond)
        def forward(number=number, out=out):
            read(number, pool.at[0]).wait()
            write(number, out).start()

    for number, out, here, beyond, *_ in routes:
        pl.when(here | beyond)(lambda n=number, out=out: write(n, out).wait())


def neighbour_states(asked, pool, from_x, from_y, place):
    return pl.pallas_call(
        state_kernel,
        out_shape=[jax.ShapeDtypeStruct(pool.shape[1:], pool.dtype)] * 2,
        in_specs=[SMEM, SMEM, HBM, HBM, HBM],
        out_specs=[HBM, HBM],
        scratch_shapes=[
            pltpu.VMEM((2,) + pool.shape[1:], pool.dtype),
            pltpu.SemaphoreType.DMA((2,)),
            pltpu.SemaphoreType.DMA((2,)),
        ],
        compiler_params=params(WHOLE),
        cost_estimate=pl.CostEstimate(flops=0, bytes_accessed=2**20, transcendentals=0),
    )(place, asked, pool, from_x, from_y)


def dot_nt(a, b):
    return lax.dot_general(a, b, (((1,), (1,)), ((), ())), preferred_element_type=F32)


def suffix_kernel(q, k, v, acc, stats):
    rows, group = q.shape[0], q.shape[1] // HEAD_DIM
    stacked = jnp.concatenate([q[:, g * HEAD_DIM : (g + 1) * HEAD_DIM] for g in range(group)], axis=0)
    shape = (rows, group * rows)
    query = lax.rem(lax.broadcasted_iota(jnp.int32, shape, 1), rows)
    seen = lax.broadcasted_iota(jnp.int32, shape, 0) <= query
    scores = jnp.where(seen, dot_nt(k[...], stacked), -1e30)
    top = jnp.max(scores, axis=0, keepdims=True)
    weights = jnp.exp2((scores - top) * SCALE2)
    total = jnp.sum(weights, axis=0, keepdims=True)
    mixed = jnp.dot(v[...].T, weights.astype(BF16), preferred_element_type=F32)
    for g in range(group):
        cols = slice(g * rows, (g + 1) * rows)
        acc[g * HEAD_DIM : (g + 1) * HEAD_DIM] = mixed[:, cols]
        stats[0, g : g + 1] = top[:, cols]
        stats[0, group + g : group + g + 1] = total[:, cols]


def suffix_attention(queries, new_kv):
    rows, width = queries.shape
    span = width // KV_HEADS
    lines = 2 * span // HEAD_DIM
    return pl.pallas_call(
        suffix_kernel,
        grid=(KV_HEADS,),
        out_shape=[
            jax.ShapeDtypeStruct((ROOM * width, rows), F32),
            jax.ShapeDtypeStruct((KV_HEADS, lines, rows), F32),
        ],
        in_specs=[
            pl.BlockSpec((rows, span), lambda i: (0, i)),
            pl.BlockSpec((rows, HEAD_DIM), lambda i: (0, i)),
            pl.BlockSpec((rows, HEAD_DIM), lambda i: (0, KV_HEADS + i)),
        ],
        out_specs=[
            pl.BlockSpec((span, rows), lambda i: (i, 0)),
            pl.BlockSpec((1, lines, rows), lambda i: (i, 0, 0)),
        ],
        compiler_params=params(WHOLE),
        cost_estimate=pl.CostEstimate(
            flops=4 * rows * rows * width, bytes_accessed=8 * rows * width, transcendentals=rows * rows * 32
        ),
    )(queries, new_kv, new_kv)


def prefix_kernel(
    holder, count, q, stats, acc_hbm, arrived, out, kv, res, acc, k_sem, v_sem, acc_sem, out_sem
):
    hits, blk = holder.shape[1], arrived.shape[1]
    rows, width = q.shape
    span, keys, half = width // KV_HEADS, hits * blk, KV_HEADS * HEAD_DIM
    group = span // HEAD_DIM

    def from_holder(j, side, sem):
        source = jnp.where(j < count[0, 0], holder[0, j], holder[0, 0])
        cols = pl.ds(side * half, half)
        return pltpu.make_async_copy(arrived.at[source, :, cols], kv.at[pl.ds(j * blk, blk), cols], sem.at[j])

    def suffix_of(k):
        lines = pl.ds(k * span, span)
        return pltpu.make_async_copy(acc_hbm.at[lines], acc.at[lines], acc_sem.at[k])

    for j in range(hits):
        from_holder(j, 0, k_sem).start()
    for j in range(hits):
        from_holder(j, 1, v_sem).start()
    for k in range(KV_HEADS):
        suffix_of(k).start()
    sure = hits // 2 * blk
    live = lax.broadcasted_iota(jnp.int32, (keys - sure, 1), 0) < count[0, 0] * blk - sure
    for j in range(hits):
        from_holder(j, 0, k_sem).wait()

    def scores_of(k):
        stacked = [q[:, k * span + g * HEAD_DIM : k * span + (g + 1) * HEAD_DIM] for g in range(group)]
        return dot_nt(kv[:, k * HEAD_DIM : (k + 1) * HEAD_DIM], jnp.concatenate(stacked, axis=0))

    later = scores_of(0)
    sends = []
    for k in range(KV_HEADS):
        scores = jnp.concatenate([later[:sure], jnp.where(live, later[sure:], -1e30)], axis=0)
        if k + 1 < KV_HEADS:
            later = scores_of(k + 1)
        old = jnp.concatenate([stats[k, g : g + 1] for g in range(group)], axis=1)
        before = jnp.concatenate([stats[k, group + g : group + g + 1] for g in range(group)], axis=1)
        top = jnp.maximum(old, jnp.max(scores, axis=0, keepdims=True))
        weights = jnp.exp2((scores - top) * SCALE2)
        keep = jnp.exp2((old - top) * SCALE2)
        total = keep * before + jnp.sum(weights, axis=0, keepdims=True)
        if k == 0:
            for j in range(hits):
                from_holder(j, 1, v_sem).wait()
        head_values = kv[:, half + k * HEAD_DIM : half + (k + 1) * HEAD_DIM]
        mixed = jnp.dot(head_values.T, weights.astype(BF16), preferred_element_type=F32)
        inverse = 1.0 / total
        kept = keep * inverse
        suffix_of(k).wait()
        for g in range(group):
            lines = slice(k * span + g * HEAD_DIM, k * span + (g + 1) * HEAD_DIM)
            cols = slice(g * rows, (g + 1) * rows)
            both = kept[:, cols] * acc[lines] + inverse[:, cols] * mixed[:, cols]
            res[:, lines] = both.T.astype(BF16)
        cols = pl.ds(k * span, span)
        sends.append(pltpu.make_async_copy(res.at[:, cols], out.at[:, cols], out_sem.at[k]))
        sends[-1].start()
    for copy in sends:
        copy.wait()


def prefix_attention(queries, acc, stats, arrived, hit_holder, hit_count):
    rows, width = queries.shape
    blk, kv_width = arrived.shape[1:]
    hits = hit_holder.shape[1]
    keys = hits * blk
    dma = pltpu.SemaphoreType.DMA
    return pl.pallas_call(
        prefix_kernel,
        out_shape=jax.ShapeDtypeStruct((rows, width), BF16),
        in_specs=[SMEM, SMEM, VMEM, VMEM, HBM, HBM],
        out_specs=HBM,
        scratch_shapes=[
            pltpu.VMEM((keys, kv_width), BF16),
            pltpu.VMEM((rows, width), BF16),
            pltpu.VMEM((width, rows), F32),
            dma((hits,)),
            dma((hits,)),
            dma((KV_HEADS,)),
            dma((KV_HEADS,)),
        ],
        compiler_params=params(40 * MIB),
        cost_estimate=pl.CostEstimate(
            flops=4 * rows * keys * width, bytes_accessed=8 * rows * width, transcendentals=rows * keys * 32
        ),
    )(hit_holder, hit_count.reshape(1, 1), queries, stats, acc, arrived)


def two_parts(value):
    high = value.astype(BF16)
    return high, (value - high.astype(F32)).astype(BF16)


def spread_of(heads, tile):
    first = pl.program_id(0) * (tile // SSM_HEAD_DIM)
    head_of = lax.broadcasted_iota(jnp.int32, (heads, tile), 1) // SSM_HEAD_DIM + first
    same = lax.broadcasted_iota(jnp.int32, (heads, tile), 0) == head_of
    spread = same.astype(F32).astype(BF16)
    return jnp.concatenate([spread, spread], axis=0)


def mixer_kernel(choice, slot, x, step, rate, into, outof, gain, *rest):
    pools, states = rest[:3], rest[3:-6]
    y, wide, inner, carried, start, sem = rest[-6:]
    rows, heads = step.shape
    index = pl.program_id(0)

    @pl.when(index == 0)
    def prepare():
        sources = [pool.at[slot[0]] for pool in pools] + list(states)
        for shift, source in enumerate(sources):

            @pl.when(choice[0] == shift)
            def fetch(source=source):
                pltpu.make_async_copy(source, start, sem).start()

        lower = lax.broadcasted_iota(jnp.int32, (rows, rows), 0) >= lax.broadcasted_iota(
            jnp.int32, (rows, rows), 1
        )
        decay = jnp.dot(
            lower.astype(F32), -rate[...] * step[...], precision=lax.Precision.HIGHEST,
            preferred_element_type=F32,
        )
        rise = jnp.exp(decay)
        fall = jnp.exp(-decay) * step[...]
        wide[:rows, :heads], wide[:rows, heads:] = two_parts(rise)
        wide[rows : 2 * rows, :heads], wide[rows : 2 * rows, heads:] = two_parts(fall)
        gains = jnp.broadcast_to(gain[...], (16, heads))
        wide[2 * rows :, :heads], wide[2 * rows :, heads:] = two_parts(gains)
        cross = lax.dot_general(
            outof[...], into[...], (((1,), (1,)), ((), ())),
            precision=lax.Precision.HIGHEST, preferred_element_type=F32,
        )
        high, low = two_parts(jnp.where(lower, cross, 0.0))
        inner[:, :rows] = high
        inner[:, rows : 2 * rows] = high
        inner[:, 2 * rows :] = low
        high, low = two_parts(outof[...])
        carried[...] = jnp.concatenate([high, high, low], axis=1)
        pltpu.make_async_copy(pools[0].at[0], start, sem).wait()

    tile = x.shape[1]
    spread = spread_of(heads, tile)
    expanded = jnp.dot(wide[...], spread, preferred_element_type=F32)
    values = x[...].astype(F32)
    high, low = two_parts(expanded[rows : 2 * rows] * values)
    total = jnp.dot(
        inner[...], jnp.concatenate([high, low, high], axis=0), preferred_element_type=F32
    )
    first = start[:, pl.ds(pl.multiple_of(index * tile, tile), tile)]
    high, low = two_parts(first)
    total = total + jnp.dot(
        carried[...], jnp.concatenate([high, low, high], axis=0), preferred_element_type=F32
    )
    y[...] = (expanded[:rows] * total + expanded[2 * rows : 2 * rows + 1] * values).astype(BF16)


def mixer(choice, slot, ssm_input, step_size, decay_rate, state_in, state_out, skip_gain, pools, states):
    rows, channels = ssm_input.shape
    heads, ns = decay_rate.shape[0], state_in.shape[1]
    whole = lambda shape: pl.BlockSpec(shape, lambda i: (0,) * len(shape))
    return pl.pallas_call(
        mixer_kernel,
        grid=(channels // TILE,),
        out_shape=jax.ShapeDtypeStruct((rows, channels), BF16),
        in_specs=[
            SMEM,
            SMEM,
            pl.BlockSpec((rows, TILE), lambda i: (0, i)),
            whole((rows, heads)),
            whole((1, heads)),
            whole((rows, ns)),
            whole((rows, ns)),
            whole((1, heads)),
        ]
        + [HBM] * (len(pools) + len(states)),
        out_specs=pl.BlockSpec((rows, TILE), lambda i: (0, i)),
        scratch_shapes=[
            pltpu.VMEM((2 * rows + 16, 2 * heads), BF16),
            pltpu.VMEM((rows, 3 * rows), BF16),
            pltpu.VMEM((rows, 3 * ns), BF16),
            pltpu.VMEM((ns, channels), F32),
            pltpu.SemaphoreType.DMA,
        ],
        compiler_params=params(56 * MIB),
        cost_estimate=pl.CostEstimate(
            flops=12 * rows * rows * channels, bytes_accessed=4 * rows * channels, transcendentals=0
        ),
    )(
        choice, slot, ssm_input, step_size, decay_rate[None, :], state_in, state_out, skip_gain[None, :], *pools, *states
    )


def body(
    queries,
    new_kv,
    kv_pool,
    hit_holder,
    hit_block,
    hit_count,
    ssm_input,
    step_size,
    decay_rate,
    state_in,
    state_out,
    skip_gain,
    state_pool,
    state_group,
    state_slot,
):
    n_grp, n_dev = lax.axis_size("grp"), lax.axis_size("dev")
    own_group = lax.axis_index("grp").astype(jnp.int32)
    own_dev = lax.axis_index("dev").astype(jnp.int32)
    place = jnp.stack([own_group, own_dev, jnp.int32(n_dev)])
    slots = state_pool.shape[0]
    early = slots - slots // 2

    def swap(value, by):
        return lax.ppermute(value, "grp", [(i, i ^ by) for i in range(n_grp)])

    near = n_grp == 4 and slots > 1
    requests = make_requests(hit_holder, hit_block, hit_count, state_group, state_slot, n_grp * n_dev, slots)
    asked = lax.all_to_all(requests, AXES, split_axis=0, concat_axis=0, tiled=True)
    if near:
        from_x, from_y = swap(state_pool[:early], 1), swap(state_pool[early:], 2)
        asked, from_x, from_y = lax.optimization_barrier((asked, from_x, from_y))
    picked = pick_blocks(asked, kv_pool)
    arrived = lax.all_to_all(picked, AXES, split_axis=0, concat_axis=0, tiled=True)
    if near:
        out_x, out_y = neighbour_states(asked, state_pool, from_x, from_y, place)
        pools, states = (state_pool, from_x, from_y), (swap(out_x, 1), swap(out_y, 2))
        first = state_slot < early
        step = lax.bitwise_xor(own_group, state_group)
        far = jnp.where(first, jnp.where(step == 1, 1, 4), jnp.where(step == 2, 2, 3))
        choice = jnp.where(step == 0, 0, far)
        slot = jnp.where(choice == 2, state_slot - early, state_slot)
    else:
        everyone = lax.all_gather(state_pool, "grp", axis=0, tiled=True)
        pools, states = (everyone,) * 3, ()
        choice, slot = jnp.zeros_like(state_slot), state_group * slots + state_slot
    acc, stats = suffix_attention(queries, new_kv)
    mixed = mixer(
        choice, slot, ssm_input, step_size, decay_rate, state_in, state_out, skip_gain, pools, states
    )
    attended = prefix_attention(queries, acc, stats, arrived, hit_holder, hit_count)
    return (attended, mixed)


def solution(mesh):
    spread = P(AXES, None)
    spread3 = P(AXES, None, None)
    line = P(AXES)
    return jax.shard_map(
        body,
        mesh=mesh,
        in_specs=(
            spread,
            spread,
            spread3,
            spread,
            spread,
            line,
            spread,
            spread,
            P(),
            spread,
            spread,
            P(),
            spread3,
            line,
            line,
        ),
        out_specs=(spread, spread),
        check_vma=False,
    )
```

```python
import functools

import jax
import jax.numpy as jnp
from jax import lax
from jax.experimental import pallas as pl
from jax.experimental.pallas import tpu as pltpu
from jax.sharding import PartitionSpec as P

KV_HEADS = 8
HEAD_DIM = 128
SSM_HEAD_DIM = 64
LANES = 128
TILE = 1024
AXES = ("grp", "dev")
SCALE2 = HEAD_DIM ** (-0.5) * 1.4426950408889634
SMEM = pl.BlockSpec(memory_space=pltpu.SMEM)
VMEM = pl.BlockSpec(memory_space=pltpu.VMEM)
HBM = pl.BlockSpec(memory_space=pltpu.HBM)
MIB = 2**20
ROOM = 8
WHOLE = 56 * MIB
F32 = jnp.float32
BF16 = jnp.bfloat16


def params(limit):
    return pltpu.CompilerParams(vmem_limit_bytes=limit)


def request_kernel(slots, holder, block, count, group, slot, out):
    shape = (out.shape[0], holder.shape[1])
    rows = lax.broadcasted_iota(jnp.int32, shape, 0)
    entries = lax.broadcasted_iota(jnp.int32, shape, 1)
    chosen = (rows == holder[...]) & (entries < count[...])
    code = jnp.sum(jnp.where(chosen, block[...] + 1, 0), axis=1, keepdims=True)
    lanes = lax.broadcasted_iota(jnp.int32, out.shape, 1)
    out[...] = jnp.where(lanes == 0, code, group[...] * slots + slot[...])


def make_requests(hit_holder, hit_block, hit_count, state_group, state_slot, n_all, slots):
    one = lambda value: value.reshape(1, 1)
    return pl.pallas_call(
        functools.partial(request_kernel, slots),
        out_shape=jax.ShapeDtypeStruct((n_all, LANES), jnp.int32),
        in_specs=[VMEM] * 5,
        out_specs=VMEM,
    )(hit_holder, hit_block, one(hit_count), one(state_group), one(state_slot))


def pick_kernel(asked, pool, out, held, in_sem, out_sem):
    n = out.shape[0]

    def read(i):
        return pltpu.make_async_copy(pool.at[jnp.maximum(asked[i, 0] - 1, 0)], held.at[i], in_sem.at[i])

    def write(i):
        return pltpu.make_async_copy(held.at[i], out.at[i], out_sem.at[i])

    for i in range(n):
        pl.when(asked[i, 0] > 0)(lambda i=i: read(i).start())
    for i in range(n):

        @pl.when(asked[i, 0] > 0)
        def forward(i=i):
            read(i).wait()
            write(i).start()

    for i in range(n):
        pl.when(asked[i, 0] > 0)(lambda i=i: write(i).wait())


def pick_blocks(asked, pool):
    n = asked.shape[0]
    shape = (n,) + pool.shape[1:]
    return pl.pallas_call(
        pick_kernel,
        out_shape=jax.ShapeDtypeStruct(shape, pool.dtype),
        in_specs=[SMEM, HBM],
        out_specs=HBM,
        scratch_shapes=[
            pltpu.VMEM(shape, pool.dtype),
            pltpu.SemaphoreType.DMA((n,)),
            pltpu.SemaphoreType.DMA((n,)),
        ],
        compiler_params=params(WHOLE),
        cost_estimate=pl.CostEstimate(flops=0, bytes_accessed=4 * n * 65536, transcendentals=0),
    )(asked, pool)


def state_kernel(place, asked, pool, from_x, from_y, out_x, out_y, held, in_sem, out_sem):
    slots, early, own = pool.shape[0], from_x.shape[0], place[0]
    routes = []
    for number, (by, out) in enumerate(((1, out_x), (2, out_y))):
        code = asked[lax.bitwise_xor(own, by) * place[2] + place[1], 1]
        group, slot = lax.div(code, slots), lax.rem(code, slots)
        over_x = by == 1
        fits = slot >= early if over_x else slot < early
        here = fits & (group == own)
        beyond = fits & (group == lax.bitwise_xor(own, 3 - by))
        there, at = (from_y, slot - early) if over_x else (from_x, slot)
        routes.append((number, out, here, beyond, slot, there, at))

    def read(number, source):
        return pltpu.make_async_copy(source, held.at[number], in_sem.at[number])

    def write(number, out):
        return pltpu.make_async_copy(held.at[number], out, out_sem.at[number])

    for number, out, here, beyond, slot, there, at in routes:
        pl.when(here)(lambda n=number, slot=slot: read(n, pool.at[slot]).start())
        pl.when(beyond)(lambda n=number, there=there, at=at: read(n, there.at[at]).start())
    for number, out, here, beyond, *_ in routes:

        @pl.when(here | beyond)
        def forward(number=number, out=out):
            read(number, pool.at[0]).wait()
            write(number, out).start()

    for number, out, here, beyond, *_ in routes:
        pl.when(here | beyond)(lambda n=number, out=out: write(n, out).wait())


def neighbour_states(asked, pool, from_x, from_y, place):
    return pl.pallas_call(
        state_kernel,
        out_shape=[jax.ShapeDtypeStruct(pool.shape[1:], pool.dtype)] * 2,
        in_specs=[SMEM, SMEM, HBM, HBM, HBM],
        out_specs=[HBM, HBM],
        scratch_shapes=[
            pltpu.VMEM((2,) + pool.shape[1:], pool.dtype),
            pltpu.SemaphoreType.DMA((2,)),
            pltpu.SemaphoreType.DMA((2,)),
        ],
        compiler_params=params(WHOLE),
        cost_estimate=pl.CostEstimate(flops=0, bytes_accessed=2**20, transcendentals=0),
    )(place, asked, pool, from_x, from_y)


def dot_nt(a, b):
    return lax.dot_general(a, b, (((1,), (1,)), ((), ())), preferred_element_type=F32)


def suffix_kernel(q, k, v, acc, stats):
    rows, group = q.shape[0], q.shape[1] // HEAD_DIM
    stacked = jnp.concatenate([q[:, g * HEAD_DIM : (g + 1) * HEAD_DIM] for g in range(group)], axis=0)
    shape = (rows, group * rows)
    query = lax.rem(lax.broadcasted_iota(jnp.int32, shape, 1), rows)
    seen = lax.broadcasted_iota(jnp.int32, shape, 0) <= query
    scores = jnp.where(seen, dot_nt(k[...], stacked), -1e30)
    top = jnp.max(scores, axis=0, keepdims=True)
    weights = jnp.exp2((scores - top) * SCALE2)
    total = jnp.sum(weights, axis=0, keepdims=True)
    mixed = jnp.dot(v[...].T, weights.astype(BF16), preferred_element_type=F32)
    for g in range(group):
        cols = slice(g * rows, (g + 1) * rows)
        acc[g * HEAD_DIM : (g + 1) * HEAD_DIM] = mixed[:, cols]
        stats[0, g : g + 1] = top[:, cols]
        stats[0, group + g : group + g + 1] = total[:, cols]


def suffix_attention(queries, new_kv):
    rows, width = queries.shape
    span = width // KV_HEADS
    lines = 2 * span // HEAD_DIM
    return pl.pallas_call(
        suffix_kernel,
        grid=(KV_HEADS,),
        out_shape=[
            jax.ShapeDtypeStruct((ROOM * width, rows), F32),
            jax.ShapeDtypeStruct((KV_HEADS, lines, rows), F32),
        ],
        in_specs=[
            pl.BlockSpec((rows, span), lambda i: (0, i)),
            pl.BlockSpec((rows, HEAD_DIM), lambda i: (0, i)),
            pl.BlockSpec((rows, HEAD_DIM), lambda i: (0, KV_HEADS + i)),
        ],
        out_specs=[
            pl.BlockSpec((span, rows), lambda i: (i, 0)),
            pl.BlockSpec((1, lines, rows), lambda i: (i, 0, 0)),
        ],
        compiler_params=params(WHOLE),
        cost_estimate=pl.CostEstimate(
            flops=4 * rows * rows * width, bytes_accessed=8 * rows * width, transcendentals=rows * rows * 32
        ),
    )(queries, new_kv, new_kv)


def prefix_kernel(
    holder, count, q, stats, acc_hbm, arrived, out, kv, res, acc, k_sem, v_sem, acc_sem, out_sem
):
    hits, blk = holder.shape[1], arrived.shape[1]
    rows, width = q.shape
    span, keys, half = width // KV_HEADS, hits * blk, KV_HEADS * HEAD_DIM
    group = span // HEAD_DIM

    def from_holder(j, side, sem):
        source = jnp.where(j < count[0, 0], holder[0, j], holder[0, 0])
        cols = pl.ds(side * half, half)
        return pltpu.make_async_copy(arrived.at[source, :, cols], kv.at[pl.ds(j * blk, blk), cols], sem.at[j])

    def suffix_of(k):
        lines = pl.ds(k * span, span)
        return pltpu.make_async_copy(acc_hbm.at[lines], acc.at[lines], acc_sem.at[k])

    for j in range(hits):
        from_holder(j, 0, k_sem).start()
    for j in range(hits):
        from_holder(j, 1, v_sem).start()
    sure = hits // 2 * blk
    live = lax.broadcasted_iota(jnp.int32, (keys - sure, 1), 0) < count[0, 0] * blk - sure
    for j in range(hits):
        from_holder(j, 0, k_sem).wait()

    def scores_of(k):
        stacked = [q[:, k * span + g * HEAD_DIM : k * span + (g + 1) * HEAD_DIM] for g in range(group)]
        return dot_nt(kv[:, k * HEAD_DIM : (k + 1) * HEAD_DIM], jnp.concatenate(stacked, axis=0))

    later = scores_of(0)
    suffix_of(0).start()
    suffix_of(1).start()
    sends = []
    for k in range(KV_HEADS):
        scores = jnp.concatenate([later[:sure], jnp.where(live, later[sure:], -1e30)], axis=0)
        if k + 1 < KV_HEADS:
            later = scores_of(k + 1)
        old = jnp.concatenate([stats[k, g : g + 1] for g in range(group)], axis=1)
        before = jnp.concatenate([stats[k, group + g : group + g + 1] for g in range(group)], axis=1)
        top = jnp.maximum(old, jnp.max(scores, axis=0, keepdims=True))
        weights = jnp.exp2((scores - top) * SCALE2)
        keep = jnp.exp2((old - top) * SCALE2)
        total = keep * before + jnp.sum(weights, axis=0, keepdims=True)
        if k == 0:
            for j in range(hits):
                from_holder(j, 1, v_sem).wait()
        head_values = kv[:, half + k * HEAD_DIM : half + (k + 1) * HEAD_DIM]
        mixed = jnp.dot(head_values.T, weights.astype(BF16), preferred_element_type=F32)
        inverse = 1.0 / total
        kept = keep * inverse
        suffix_of(k).wait()
        if k + 2 < KV_HEADS:
            suffix_of(k + 2).start()
        for g in range(group):
            lines = slice(k * span + g * HEAD_DIM, k * span + (g + 1) * HEAD_DIM)
            cols = slice(g * rows, (g + 1) * rows)
            both = kept[:, cols] * acc[lines] + inverse[:, cols] * mixed[:, cols]
            res[:, lines] = both.T.astype(BF16)
        cols = pl.ds(k * span, span)
        sends.append(pltpu.make_async_copy(res.at[:, cols], out.at[:, cols], out_sem.at[k]))
        sends[-1].start()
    for copy in sends:
        copy.wait()


def prefix_attention(queries, acc, stats, arrived, hit_holder, hit_count):
    rows, width = queries.shape
    blk, kv_width = arrived.shape[1:]
    hits = hit_holder.shape[1]
    keys = hits * blk
    dma = pltpu.SemaphoreType.DMA
    return pl.pallas_call(
        prefix_kernel,
        out_shape=jax.ShapeDtypeStruct((rows, width), BF16),
        in_specs=[SMEM, SMEM, VMEM, VMEM, HBM, HBM],
        out_specs=HBM,
        scratch_shapes=[
            pltpu.VMEM((keys, kv_width), BF16),
            pltpu.VMEM((rows, width), BF16),
            pltpu.VMEM((width, rows), F32),
            dma((hits,)),
            dma((hits,)),
            dma((KV_HEADS,)),
            dma((KV_HEADS,)),
        ],
        compiler_params=params(40 * MIB),
        cost_estimate=pl.CostEstimate(
            flops=4 * rows * keys * width, bytes_accessed=8 * rows * width, transcendentals=rows * keys * 32
        ),
    )(hit_holder, hit_count.reshape(1, 1), queries, stats, acc, arrived)


def two_parts(value):
    high = value.astype(BF16)
    return high, (value - high.astype(F32)).astype(BF16)


def spread_of(heads, tile):
    first = pl.program_id(0) * (tile // SSM_HEAD_DIM)
    head_of = lax.broadcasted_iota(jnp.int32, (heads, tile), 1) // SSM_HEAD_DIM + first
    same = lax.broadcasted_iota(jnp.int32, (heads, tile), 0) == head_of
    spread = same.astype(F32).astype(BF16)
    return jnp.concatenate([spread, spread], axis=0)


def mixer_kernel(choice, slot, x, step, rate, into, outof, gain, *rest):
    pools, states = rest[:3], rest[3:-6]
    y, wide, inner, carried, start, sem = rest[-6:]
    rows, heads = step.shape
    index = pl.program_id(0)

    @pl.when(index == 0)
    def prepare():
        sources = [pool.at[slot[0]] for pool in pools] + list(states)
        for shift, source in enumerate(sources):

            @pl.when(choice[0] == shift)
            def fetch(source=source):
                pltpu.make_async_copy(source, start, sem).start()

        lower = lax.broadcasted_iota(jnp.int32, (rows, rows), 0) >= lax.broadcasted_iota(
            jnp.int32, (rows, rows), 1
        )
        decay = jnp.dot(
            lower.astype(F32), -rate[...] * step[...], precision=lax.Precision.HIGHEST,
            preferred_element_type=F32,
        )
        rise = jnp.exp(decay)
        fall = jnp.exp(-decay) * step[...]
        wide[:rows, :heads], wide[:rows, heads:] = two_parts(rise)
        wide[rows : 2 * rows, :heads], wide[rows : 2 * rows, heads:] = two_parts(fall)
        gains = jnp.broadcast_to(gain[...], (16, heads))
        wide[2 * rows :, :heads], wide[2 * rows :, heads:] = two_parts(gains)
        cross = lax.dot_general(
            outof[...], into[...], (((1,), (1,)), ((), ())),
            precision=lax.Precision.HIGHEST, preferred_element_type=F32,
        )
        high, low = two_parts(jnp.where(lower, cross, 0.0))
        inner[:, :rows] = high
        inner[:, rows : 2 * rows] = high
        inner[:, 2 * rows :] = low
        high, low = two_parts(outof[...])
        carried[...] = jnp.concatenate([high, high, low], axis=1)
        pltpu.make_async_copy(pools[0].at[0], start, sem).wait()

    tile = x.shape[1]
    spread = spread_of(heads, tile)
    expanded = jnp.dot(wide[...], spread, preferred_element_type=F32)
    values = x[...].astype(F32)
    high, low = two_parts(expanded[rows : 2 * rows] * values)
    total = jnp.dot(
        inner[...], jnp.concatenate([high, low, high], axis=0), preferred_element_type=F32
    )
    first = start[:, pl.ds(pl.multiple_of(index * tile, tile), tile)]
    high, low = two_parts(first)
    total = total + jnp.dot(
        carried[...], jnp.concatenate([high, low, high], axis=0), preferred_element_type=F32
    )
    y[...] = (expanded[:rows] * total + expanded[2 * rows : 2 * rows + 1] * values).astype(BF16)


def mixer(choice, slot, ssm_input, step_size, decay_rate, state_in, state_out, skip_gain, pools, states):
    rows, channels = ssm_input.shape
    heads, ns = decay_rate.shape[0], state_in.shape[1]
    whole = lambda shape: pl.BlockSpec(shape, lambda i: (0,) * len(shape))
    return pl.pallas_call(
        mixer_kernel,
        grid=(channels // TILE,),
        out_shape=jax.ShapeDtypeStruct((rows, channels), BF16),
        in_specs=[
            SMEM,
            SMEM,
            pl.BlockSpec((rows, TILE), lambda i: (0, i)),
            whole((rows, heads)),
            whole((1, heads)),
            whole((rows, ns)),
            whole((rows, ns)),
            whole((1, heads)),
        ]
        + [HBM] * (len(pools) + len(states)),
        out_specs=pl.BlockSpec((rows, TILE), lambda i: (0, i)),
        scratch_shapes=[
            pltpu.VMEM((2 * rows + 16, 2 * heads), BF16),
            pltpu.VMEM((rows, 3 * rows), BF16),
            pltpu.VMEM((rows, 3 * ns), BF16),
            pltpu.VMEM((ns, channels), F32),
            pltpu.SemaphoreType.DMA,
        ],
        compiler_params=params(56 * MIB),
        cost_estimate=pl.CostEstimate(
            flops=12 * rows * rows * channels, bytes_accessed=4 * rows * channels, transcendentals=0
        ),
    )(
        choice, slot, ssm_input, step_size, decay_rate[None, :], state_in, state_out, skip_gain[None, :], *pools, *states
    )


def body(
    queries,
    new_kv,
    kv_pool,
    hit_holder,
    hit_block,
    hit_count,
    ssm_input,
    step_size,
    decay_rate,
    state_in,
    state_out,
    skip_gain,
    state_pool,
    state_group,
    state_slot,
):
    n_grp, n_dev = lax.axis_size("grp"), lax.axis_size("dev")
    own_group = lax.axis_index("grp").astype(jnp.int32)
    own_dev = lax.axis_index("dev").astype(jnp.int32)
    place = jnp.stack([own_group, own_dev, jnp.int32(n_dev)])
    slots = state_pool.shape[0]
    early = slots - slots // 2

    def swap(value, by):
        return lax.ppermute(value, "grp", [(i, i ^ by) for i in range(n_grp)])

    near = n_grp == 4 and slots > 1
    requests = make_requests(hit_holder, hit_block, hit_count, state_group, state_slot, n_grp * n_dev, slots)
    asked = lax.all_to_all(requests, AXES, split_axis=0, concat_axis=0, tiled=True)
    if near:
        from_x, from_y = swap(state_pool[:early], 1), swap(state_pool[early:], 2)
        asked, from_x, from_y = lax.optimization_barrier((asked, from_x, from_y))
    picked = pick_blocks(asked, kv_pool)
    arrived = lax.all_to_all(picked, AXES, split_axis=0, concat_axis=0, tiled=True)
    if near:
        out_x, out_y = neighbour_states(asked, state_pool, from_x, from_y, place)
        pools, states = (state_pool, from_x, from_y), (swap(out_x, 1), swap(out_y, 2))
        first = state_slot < early
        step = lax.bitwise_xor(own_group, state_group)
        far = jnp.where(first, jnp.where(step == 1, 1, 4), jnp.where(step == 2, 2, 3))
        choice = jnp.where(step == 0, 0, far)
        slot = jnp.where(choice == 2, state_slot - early, state_slot)
    else:
        everyone = lax.all_gather(state_pool, "grp", axis=0, tiled=True)
        pools, states = (everyone,) * 3, ()
        choice, slot = jnp.zeros_like(state_slot), state_group * slots + state_slot
    acc, stats = suffix_attention(queries, new_kv)
    mixed = mixer(
        choice, slot, ssm_input, step_size, decay_rate, state_in, state_out, skip_gain, pools, states
    )
    attended = prefix_attention(queries, acc, stats, arrived, hit_holder, hit_count)
    return (attended, mixed)


def solution(mesh):
    spread = P(AXES, None)
    spread3 = P(AXES, None, None)
    line = P(AXES)
    return jax.shard_map(
        body,
        mesh=mesh,
        in_specs=(
            spread,
            spread,
            spread3,
            spread,
            spread,
            line,
            spread,
            spread,
            P(),
            spread,
            spread,
            P(),
            spread3,
            line,
            line,
        ),
        out_specs=(spread, spread),
        check_vma=False,
    )
```
